32 devices in a mesh: row: 8 (over z, x), col: 4 (over y, core).
Axes of the slice: x: 2, y: 2, z: 4, core: 2. Of those that a mesh axis runs over, the one named last changes fastest.
Arguments:
- psi: bfloat16 [1024, 16, 512], P('row', None, 'col'), may hold values from -6 to 6
- env_left: bfloat16 [8, 3, 128, 128, 34], P('row'), may hold values from -0.0546875 to 0.0546875
- env_right: bfloat16 [4, 3, 128, 34, 128], P('col'), may hold values from -0.3125 to 0.3125
- first_site_operator: bfloat16 [34, 34, 4, 4], replicated, may hold values from -0.5 to 0.5
- mpo_right: bfloat16 [34, 34, 4, 4], replicated, may hold values from -0.5 to 0.5
- block_mask: int32 [8, 4], P('row', 'col'), may hold values 0 or 1
- left_live: int32 [8], P('row'), may hold values from 64 to 128, as said below
- right_live: int32 [4], P('col'), may hold values from 64 to 128, as said below
Outputs:
- hpsi: bfloat16 [1024, 16, 512], P('row', None, 'col')
- residual: bfloat16 [1024, 16, 512], P('row', None, 'col')
- quotient: float32 [], replicated
The draws below stay inside these ranges and needn't reach their ends.
Inputs may be any that keep to these rules, and one draw needn't show every extreme that they name: `left_live`: a block is either full or is the last block of a sector with fewer live states; some block is full. `right_live`: a block is either full or is the last block of a sector with fewer live states; some block is full.
All inputs are finite; a program needn't handle non-finite values. No bound on the sum of `block_mask` on one device may be relied on, other than what follows from the above.
Results may differ from the reference program's by a relative error of at most 0.0064.
Values may be sent and summed in bfloat16 or wider, within the bound.
A program may use at most 192 MiB of HBM per device.

```python
import jax
import jax.numpy as jnp
from jax import lax

W = 34
D4 = 4
SB = 128
P_SIZE = 16
NA = 8
NB = 4
LEFT_BOND_STATES = 1024
BOND_R = 512


def draw_sector_rows(key, amount):
    boundary = jax.random.randint(jax.random.fold_in(key, 1), (amount,), 0, 2)
    ragged = jax.random.randint(jax.random.fold_in(key, 2), (amount,), SB // 2, SB)
    chosen = jax.random.randint(jax.random.fold_in(key, 3), (), 0, amount)
    step_on = jax.random.randint(jax.random.fold_in(key, 4), (), 1, amount)
    partial_index = (chosen + step_on) % amount
    positions = jnp.arange(amount)
    values = jnp.where(boundary > 0, ragged, SB)
    values = jnp.where(positions == partial_index, SB // 2, values)
    values = jnp.where(positions == chosen, SB, values)
    return values.astype(jnp.int32)


def draw_left_live(key, part):
    return draw_sector_rows(jax.random.fold_in(key, 11), NA)


def draw_right_live(key, part):
    return draw_sector_rows(jax.random.fold_in(key, 17), NB)


def set_ends(drawn, own_key, smallest, high):
    longest = drawn.shape.index(max(drawn.shape))
    spots = []
    for shift in (0, 1):
        where = [jax.random.randint(jax.random.fold_in(own_key, axis), (), 0, length) for axis, length in enumerate(drawn.shape)]
        where[longest] = (where[longest] + shift) % drawn.shape[longest]
        spots.append(tuple(where))
    return drawn.at[spots[0]].set(smallest).at[spots[1]].set(high)


def steps_of(key, shape, split, low, high):
    factor_of, own = 1.0, jax.random.fold_in(key, 6)
    for axis_at, parts in split:
        steps = jnp.exp(jax.random.uniform(jax.random.fold_in(own, axis_at), (parts,), jnp.float32, low / len(split), high / len(split)))
        factor_of = factor_of * jnp.repeat(steps, shape[axis_at] // parts).reshape([-1 if axis == axis_at else 1 for axis in range(len(shape))])
    return factor_of


def normal_values(stream_key, extent, deviation, reach, split=(), kind=jnp.bfloat16):
    values = jax.random.normal(stream_key, extent, jnp.float32) * deviation
    if len(split) > 0:
        values = steps_of(stream_key, extent, split, -0.22, 0.18) * values
    return jnp.clip(values, min=-reach, max=reach).astype(kind)


def setup_inputs(seed: int = 0) -> dict:
    splits = jax.random.split(jax.random.key(seed), 9)
    psi = normal_values(splits[0], (LEFT_BOND_STATES, P_SIZE, BOND_R), 1.0, 6.0, ((0, 8), (2, 4)))
    env_left = normal_values(splits[1], (NA, 3, SB, SB, W), (3 * SB * W) ** -0.5, 0.0546875, ((0, 8),))
    env_right = normal_values(splits[2], (NB, 3, SB, W, SB), (3 * SB) ** -0.5, 0.3125, ((0, 4),))
    first_site_operator = normal_values(splits[3], (W, W, D4, D4), (W * D4) ** -0.5, 0.5)
    mpo_right = normal_values(splits[4], (W, W, D4, D4), (W * D4) ** -0.5, 0.5)
    block_mask = set_ends((jax.random.randint(splits[5], (NA, NB), 0, 4) < 3).astype(jnp.int32), jax.random.fold_in(splits[5], 1), 0, 1)
    left_live = draw_left_live(jax.random.fold_in(splits[8], 71), 0)
    right_live = draw_right_live(jax.random.fold_in(splits[8], 71), 0)
    return dict(psi=psi, env_left=env_left, env_right=env_right, first_site_operator=first_site_operator, mpo_right=mpo_right, block_mask=block_mask, left_live=left_live, right_live=right_live)


def reference(psi, env_left, env_right, first_site_operator, mpo_right, block_mask, left_live, right_live):
    inside = jnp.arange(SB, dtype=jnp.int32)
    row_ok = (inside[None, :] < left_live[:, None]).reshape(-1)
    col_ok = (inside[None, :] < right_live[:, None]).reshape(-1)
    expanded = jnp.repeat(jnp.repeat(block_mask, SB, axis=0), SB, axis=1)
    live_mask = (expanded > 0) & row_ok[:, None] & col_ok[None, :]
    masked_wavefunction = psi * live_mask[:, None, :].astype(psi.dtype)
    padded = jnp.pad(masked_wavefunction, ((0, 0), (0, 0), (SB, SB)))
    left_blocks = LEFT_BOND_STATES // SB

    def one_column(column):
        window = lax.dynamic_slice_in_dim(padded, column * SB, 3 * SB, 2)
        right_matrix = lax.dynamic_index_in_dim(env_right, column, 0, keepdims=False).reshape(3 * SB, W * SB)

        def one_row(position):
            strip = lax.dynamic_slice_in_dim(window, position * SB, SB, 0).reshape(SB * P_SIZE, 3 * SB)
            section_one = jnp.dot(strip, right_matrix, preferred_element_type=jnp.float32).astype(jnp.bfloat16)
            section_one = section_one.reshape(SB, D4, D4, W, SB)
            second_section = jnp.einsum("mnts,xasnb->xamtb", mpo_right.astype(jnp.float32), section_one.astype(jnp.float32)).astype(jnp.bfloat16)
            third_section = jnp.einsum("dquo,woqzj->wduzj", first_site_operator.astype(jnp.float32), second_section.astype(jnp.float32)).astype(jnp.bfloat16)
            return third_section.reshape(SB * W, P_SIZE * SB)

        outcomes = lax.map(one_row, jnp.arange(left_blocks, dtype=jnp.int32))
        zero_block = jnp.zeros((1, SB * W, P_SIZE * SB), outcomes.dtype)
        framed = jnp.concatenate([zero_block, outcomes, zero_block], axis=0)

        def one_output(position):
            couplings = lax.dynamic_index_in_dim(env_left, position, 0, keepdims=False)
            running = jnp.zeros((SB, P_SIZE * SB), jnp.float32)
            for offset in range(3):
                operand = lax.dynamic_index_in_dim(framed, position + offset, 0, keepdims=False)
                running = running + jnp.dot(couplings[offset].reshape(SB, SB * W), operand, preferred_element_type=jnp.float32)
            return running.reshape(SB, P_SIZE, SB)

        results = lax.map(one_output, jnp.arange(left_blocks, dtype=jnp.int32))
        return results.reshape(LEFT_BOND_STATES, P_SIZE, SB)

    column_list = lax.map(one_column, jnp.arange(NB, dtype=jnp.int32))
    hamiltonian_times_wavefunction = jnp.transpose(column_list, (1, 2, 0, 3)).reshape(LEFT_BOND_STATES, P_SIZE, BOND_R)
    live_float = live_mask[:, None, :].astype(jnp.float32)
    applied = hamiltonian_times_wavefunction * live_float
    psi_float = masked_wavefunction.astype(jnp.float32)
    quotient = jnp.sum(psi_float * applied) / (jnp.sum(psi_float * psi_float) + 1e-6)
    return applied.astype(jnp.bfloat16), (applied - quotient * psi_float).astype(jnp.bfloat16), quotient
```

```python
import functools

import jax
import jax.numpy as jnp
from jax import lax
from jax.experimental import pallas as pl
from jax.experimental.pallas import tpu as pltpu
from jax.sharding import PartitionSpec as P

CHUNK = 16
N_PAD = 40
M_PAD = 48


def from_behind(block, axis, distance):
    devices = range(lax.axis_size(axis))
    route = [(i - distance, i) for i in devices if i - distance in devices]
    return lax.ppermute(block, axis, route)


def shared_from_behind(coupling, distance):
    share = coupling.shape[0] // lax.axis_size("col")
    own = lax.dynamic_slice_in_dim(coupling, lax.axis_index("col") * share, share, 0)
    moved = from_behind(own, "row", distance)
    return lax.all_gather(moved, "col", axis=0, tiled=True)


def right_kernel(psi_ref, env_ref, site_ref, two_ref, one):
    rows = psi_ref.shape[0]
    depth, width, inside, lanes = env_ref.shape
    sites = site_ref.shape[1] // N_PAD

    @pl.when(pl.program_id(0) == 0)
    def _():
        one[...] = jnp.zeros_like(one)

    for w in range(0, width, 2):
        env = jnp.concatenate(
            [
                jnp.concatenate([env_ref[k, w + j] for k in range(depth)], axis=0)
                for j in range(2)
            ],
            axis=1,
        )
        found = jnp.dot(psi_ref[...], env, preferred_element_type=jnp.float32)
        for j in range(2):
            one[pl.ds(w + j, rows, stride=N_PAD), :] = found[:, j * lanes : (j + 1) * lanes]

    tall = sites * N_PAD

    def pair(i, _):
        start = pl.multiple_of(i * (2 * tall), 2 * tall)
        operand = jnp.concatenate(
            [one[pl.ds(start + j * tall, tall), :].astype(jnp.bfloat16) for j in range(2)], axis=1
        )
        found = jnp.dot(
            site_ref[...], operand, preferred_element_type=jnp.float32
        ).astype(jnp.bfloat16)
        for t in range(sites):
            for j in range(2):
                spot = pl.multiple_of((i * 2 + j) * M_PAD, M_PAD)
                two_ref[t, pl.ds(spot, M_PAD), :] = found[
                    t * M_PAD : (t + 1) * M_PAD, j * lanes : (j + 1) * lanes
                ]
        return 0

    lax.fori_loop(0, rows // sites // 2, pair, 0, unroll=8)


def right_part(widened, env, site):
    rows, depth = widened.shape
    lanes = env.shape[3]
    sites = site.shape[0] // M_PAD
    states = sites * sites
    block = CHUNK * states
    tall = rows // sites * M_PAD
    return pl.pallas_call(
        right_kernel,
        grid=(rows // block,),
        in_specs=[
            pl.BlockSpec((block, depth), lambda i: (i, 0)),
            pl.BlockSpec(env.shape, lambda i: (0, 0, 0, 0)),
            pl.BlockSpec(site.shape, lambda i: (0, 0)),
        ],
        out_specs=pl.BlockSpec((sites, CHUNK * sites * M_PAD, lanes), lambda i: (0, i, 0)),
        out_shape=jax.ShapeDtypeStruct((sites, tall, lanes), jnp.bfloat16),
        scratch_shapes=[pltpu.VMEM((block * N_PAD, lanes), jnp.float32)],
        compiler_params=pltpu.CompilerParams(vmem_limit_bytes=48 * 2**20),
        cost_estimate=pl.CostEstimate(
            flops=2 * rows * depth * env.shape[1] * lanes * 2,
            bytes_accessed=2 * sites * tall * lanes,
            transcendentals=0,
        ),
        name="right_part",
    )(widened, env, site)


def left_kernel(two_ref, site_ref, env_ref, psi_ref, own_ref, sent_ref, dot_ref, three, total):
    step = pl.program_id(0)
    lanes = two_ref.shape[2]
    sites = site_ref.shape[0] // M_PAD
    tall = sites * M_PAD
    block_rows = own_ref.shape[0]

    for x in range(0, CHUNK, 2):
        operand = jnp.concatenate(
            [two_ref[0, (x + j) * tall : (x + j + 1) * tall, :] for j in range(2)], axis=1
        )
        found = jnp.dot(
            site_ref[...], operand, preferred_element_type=jnp.float32
        ).astype(jnp.bfloat16)
        for j in range(2):
            for r in range(sites):
                three[(x + j) * M_PAD : (x + j + 1) * M_PAD, r * lanes : (r + 1) * lanes] = found[
                    r * M_PAD : (r + 1) * M_PAD, j * lanes : (j + 1) * lanes
                ]
    part = jnp.dot(env_ref[...], three[...], preferred_element_type=jnp.float32)

    @pl.when(step == 0)
    def _():
        total[...] = part

    @pl.when(step > 0)
    def _():
        total[...] += part

    @pl.when(step == pl.num_programs(0) - 1)
    def _():
        whole = total[...]
        own_ref[...] = whole[:block_rows]
        sent_ref[...] = whole[block_rows:].astype(jnp.bfloat16)
        weighed = psi_ref[0].astype(jnp.float32) * whole
        dot_ref[...] = jnp.sum(weighed.reshape(-1, 8, weighed.shape[1]), axis=0)


def left_part(two, site, env, psi_rows, t):
    lanes = two.shape[2]
    sites = site.shape[0] // M_PAD
    steps = two.shape[1] // (CHUNK * sites * M_PAD)
    tall, wide = env.shape[0], sites * lanes
    block_rows = tall // 3
    return pl.pallas_call(
        left_kernel,
        grid=(steps,),
        in_specs=[
            pl.BlockSpec((1, CHUNK * sites * M_PAD, lanes), lambda i: (t, i, 0)),
            pl.BlockSpec(site.shape, lambda i: (0, 0)),
            pl.BlockSpec((tall, CHUNK * M_PAD), lambda i: (0, i)),
            pl.BlockSpec((1, tall, wide), lambda i: (t, 0, 0)),
        ],
        out_specs=[
            pl.BlockSpec((block_rows, wide), lambda i: (0, 0)),
            pl.BlockSpec((2 * block_rows, wide), lambda i: (0, 0)),
            pl.BlockSpec((8, wide), lambda i: (0, 0)),
        ],
        out_shape=[
            jax.ShapeDtypeStruct((block_rows, wide), jnp.float32),
            jax.ShapeDtypeStruct((2 * block_rows, wide), jnp.bfloat16),
            jax.ShapeDtypeStruct((8, wide), jnp.float32),
        ],
        scratch_shapes=[
            pltpu.VMEM((CHUNK * M_PAD, wide), jnp.bfloat16),
            pltpu.VMEM((tall, wide), jnp.float32),
        ],
        compiler_params=pltpu.CompilerParams(vmem_limit_bytes=40 * 2**20),
        cost_estimate=pl.CostEstimate(
            flops=2 * tall * env.shape[1] * wide * 2,
            bytes_accessed=2 * two.shape[1] * lanes + 2 * tall * env.shape[1],
            transcendentals=0,
        ),
        name="left_part",
    )(two, site, env, psi_rows)


def sum_kernel(sizes, value_ref, out_ref, col_slots, row_slots, sems, recv_sems):
    rows, cols = sizes
    row, col = lax.axis_index("row"), lax.axis_index("col")
    peers = [((row, lax.rem(col + d, cols)), col_slots, d) for d in range(1, cols)]
    others = [((lax.rem(row + d, rows), col), row_slots, d) for d in range(1, rows)]
    barrier = pltpu.get_barrier_semaphore()
    for place, _, _ in peers + others:
        pl.semaphore_signal(barrier, inc=1, device_id=place, device_id_type=pl.DeviceIdType.MESH)
    pl.semaphore_wait(barrier, len(peers) + len(others))

    def exchange(group, offset):
        copies = []
        for place, slots, d in group:
            copy = pltpu.make_async_remote_copy(
                src_ref=slots.at[0],
                dst_ref=slots.at[d],
                send_sem=sems.at[offset + d],
                recv_sem=recv_sems.at[offset + d],
                device_id=place,
                device_id_type=pl.DeviceIdType.MESH,
            )
            copy.start()
            copies.append(copy)
        for copy in copies:
            copy.wait()

    col_slots[0] = value_ref[...]
    exchange(peers, 0)
    row_slots[0] = jnp.sum(col_slots[...], axis=0)
    exchange(others, cols)
    out_ref[...] = jnp.sum(row_slots[...], axis=0)


def sum_everywhere(value):
    rows, cols = lax.axis_size("row"), lax.axis_size("col")
    return pl.pallas_call(
        functools.partial(sum_kernel, (rows, cols)),
        out_shape=jax.ShapeDtypeStruct(value.shape, jnp.float32),
        in_specs=[pl.BlockSpec(memory_space=pltpu.VMEM)],
        out_specs=pl.BlockSpec(memory_space=pltpu.VMEM),
        scratch_shapes=[
            pltpu.VMEM((cols,) + value.shape, jnp.float32),
            pltpu.VMEM((rows,) + value.shape, jnp.float32),
            pltpu.SemaphoreType.DMA((rows + cols,)),
            pltpu.SemaphoreType.DMA((rows + cols,)),
        ],
        compiler_params=pltpu.CompilerParams(collective_id=0, has_side_effects=True),
        name="sum_everywhere",
    )(value)


def operator_matrix(tensor, narrow):
    width, sites = tensor.shape[0], tensor.shape[2]
    matrix = jnp.pad(
        jnp.transpose(tensor, (2, 0, 3, 1)),
        ((0, 0), (0, M_PAD - width), (0, 0), (0, narrow - width)),
    )
    return matrix.reshape(sites * M_PAD, sites * narrow)


def on_device(
    psi, env_left, env_right, first_site_operator, mpo_right, block_mask, left_live, right_live
):
    block_rows = env_left.shape[2]
    lanes = env_right.shape[4]
    mpo_width = env_left.shape[4]
    states = psi.shape[1]
    sites = first_site_operator.shape[2]
    inside = lax.iota(jnp.int32, block_rows)
    live = (
        (block_mask[0, 0] > 0)
        & (inside < left_live[0])[:, None]
        & (lax.iota(jnp.int32, lanes) < right_live[0])[None, :]
    )
    masked = psi * live[:, None, :].astype(jnp.bfloat16)
    low = from_behind(masked, "col", 1)
    high = from_behind(masked, "col", -1)
    env_next = shared_from_behind(env_left[0, 0], -1)
    env_prev = shared_from_behind(env_left[0, 2], 1)
    by_t = jnp.transpose(
        masked.reshape(block_rows, sites, sites, lanes), (2, 0, 1, 3)
    ).reshape(sites, block_rows, sites * lanes)
    psi_rows = jnp.concatenate(
        [by_t, from_behind(by_t, "row", -1), from_behind(by_t, "row", 1)], axis=1
    )
    widened = jnp.concatenate([low, masked, high], axis=2).reshape(
        block_rows * states, 3 * lanes
    )
    two = right_part(
        widened, jnp.transpose(env_right[0], (0, 2, 1, 3)), operator_matrix(mpo_right, N_PAD)
    )
    env_all = jnp.concatenate([env_left[0, 1], env_next, env_prev], axis=0)
    env_all = jnp.pad(env_all, ((0, 0), (0, 0), (0, M_PAD - mpo_width))).reshape(
        3 * block_rows, block_rows * M_PAD
    )
    first = operator_matrix(first_site_operator, M_PAD)
    totals, products = [], []
    for t in range(sites):
        own, sent, product = left_part(two, first, env_all, psi_rows, t)
        from_prev = from_behind(sent[:block_rows], "row", 1)
        from_next = from_behind(sent[block_rows:], "row", -1)
        totals.append((own, from_prev, from_next))
        products.append(product)
    numerator = jnp.sum(sum(products))
    masked_float = masked.astype(jnp.float32)
    denominator = jnp.sum(masked_float * masked_float)
    sums = jnp.where(lax.broadcasted_iota(jnp.int32, (8, 128), 0) < 4, numerator, denominator)
    sums = sum_everywhere(sums)
    quotient = sums[0, 0] / (sums[4, 0] + 1e-06)
    applied = jnp.stack(
        [
            (own + from_prev.astype(jnp.float32) + from_next.astype(jnp.float32)).reshape(
                block_rows, sites, lanes
            )
            for own, from_prev, from_next in totals
        ],
        axis=2,
    ).reshape(block_rows, states, lanes)
    applied = applied * live[:, None, :].astype(jnp.float32)
    return (
        applied.astype(jnp.bfloat16),
        (applied - quotient * masked_float).astype(jnp.bfloat16),
        quotient,
    )


def solution(mesh):
    return jax.shard_map(
        on_device,
        mesh=mesh,
        in_specs=(
            P("row", None, "col"),
            P("row", None, None, None, None),
            P("col", None, None, None, None),
            P(),
            P(),
            P("row", "col"),
            P("row"),
            P("col"),
        ),
        out_specs=(P("row", None, "col"), P("row", None, "col"), P()),
        check_vma=False,
    )
```

```python
import functools

import jax
import jax.numpy as jnp
from jax import lax
from jax.experimental import pallas as pl
from jax.experimental.pallas import tpu as pltpu
from jax.sharding import PartitionSpec as P

CHUNK = 16
N_PAD = 40
M_PAD = 48


def from_behind(block, axis, distance):
    devices = range(lax.axis_size(axis))
    route = [(i - distance, i) for i in devices if i - distance in devices]
    return lax.ppermute(block, axis, route)


def right_kernel(psi_ref, env_ref, site_ref, two_ref, one):
    rows = psi_ref.shape[0]
    depth, width, inside, lanes = env_ref.shape
    sites = site_ref.shape[1] // N_PAD

    @pl.when(pl.program_id(0) == 0)
    def _():
        one[...] = jnp.zeros_like(one)

    for w in range(0, width, 2):
        env = jnp.concatenate(
            [
                jnp.concatenate([env_ref[k, w + j] for k in range(depth)], axis=0)
                for j in range(2)
            ],
            axis=1,
        )
        found = jnp.dot(psi_ref[...], env, preferred_element_type=jnp.float32)
        for j in range(2):
            one[pl.ds(w + j, rows, stride=N_PAD), :] = found[:, j * lanes : (j + 1) * lanes]

    tall = sites * N_PAD

    def pair(i, _):
        start = pl.multiple_of(i * (2 * tall), 2 * tall)
        operand = jnp.concatenate(
            [one[pl.ds(start + j * tall, tall), :].astype(jnp.bfloat16) for j in range(2)], axis=1
        )
        found = jnp.dot(
            site_ref[...], operand, preferred_element_type=jnp.float32
        ).astype(jnp.bfloat16)
        for t in range(sites):
            for j in range(2):
                spot = pl.multiple_of((i * 2 + j) * M_PAD, M_PAD)
                two_ref[t, pl.ds(spot, M_PAD), :] = found[
                    t * M_PAD : (t + 1) * M_PAD, j * lanes : (j + 1) * lanes
                ]
        return 0

    lax.fori_loop(0, rows // sites // 2, pair, 0, unroll=8)


def right_part(widened, env, site):
    rows, depth = widened.shape
    lanes = env.shape[3]
    sites = site.shape[0] // M_PAD
    states = sites * sites
    block = CHUNK * states
    tall = rows // sites * M_PAD
    return pl.pallas_call(
        right_kernel,
        grid=(rows // block,),
        in_specs=[
            pl.BlockSpec((block, depth), lambda i: (i, 0)),
            pl.BlockSpec(env.shape, lambda i: (0, 0, 0, 0)),
            pl.BlockSpec(site.shape, lambda i: (0, 0)),
        ],
        out_specs=pl.BlockSpec((sites, CHUNK * sites * M_PAD, lanes), lambda i: (0, i, 0)),
        out_shape=jax.ShapeDtypeStruct((sites, tall, lanes), jnp.bfloat16),
        scratch_shapes=[pltpu.VMEM((block * N_PAD, lanes), jnp.float32)],
        compiler_params=pltpu.CompilerParams(vmem_limit_bytes=48 * 2**20),
        cost_estimate=pl.CostEstimate(
            flops=2 * rows * depth * env.shape[1] * lanes * 2,
            bytes_accessed=2 * sites * tall * lanes,
            transcendentals=0,
        ),
        name="right_part",
    )(widened, env, site)


def left_kernel(
    two_ref, site_ref, own_env_ref, far_env_ref, psi_ref,
    own_ref, next_ref, prev_ref, dot_ref, three, total,
):
    step = pl.program_id(1)
    lanes = two_ref.shape[2]
    sites = site_ref.shape[0] // M_PAD
    tall = sites * M_PAD
    block_rows = own_ref.shape[1]
    share = block_rows // lax.axis_size("col")

    for x in range(0, CHUNK, 2):
        operand = jnp.concatenate(
            [two_ref[0, (x + j) * tall : (x + j + 1) * tall, :] for j in range(2)], axis=1
        )
        found = jnp.dot(
            site_ref[...], operand, preferred_element_type=jnp.float32
        ).astype(jnp.bfloat16)
        for j in range(2):
            for r in range(sites):
                three[(x + j) * M_PAD : (x + j + 1) * M_PAD, r * lanes : (r + 1) * lanes] = found[
                    r * M_PAD : (r + 1) * M_PAD, j * lanes : (j + 1) * lanes
                ]
    env = jnp.concatenate([own_env_ref[...], far_env_ref[...]], axis=0)
    part = jnp.dot(env, three[...], preferred_element_type=jnp.float32)

    @pl.when(step == 0)
    def _():
        total[...] = part

    @pl.when(step > 0)
    def _():
        total[...] += part

    @pl.when(step == pl.num_programs(1) - 1)
    def _():
        def far(direction):
            starts = range(block_rows + direction * share, 3 * block_rows, 2 * share)
            return jnp.concatenate([total[at : at + share, :] for at in starts], axis=0)

        def psi_of(place):
            return psi_ref[0, place * block_rows : (place + 1) * block_rows, :].astype(jnp.float32)

        def folded(value):
            return jnp.sum(value.reshape(-1, 8, value.shape[1]), axis=0)

        own = total[:block_rows, :]
        to_next, to_prev = far(0), far(1)
        own_psi = psi_of(0)
        own_ref[0] = own
        next_ref[0] = to_next.astype(jnp.bfloat16)
        prev_ref[0] = to_prev.astype(jnp.bfloat16)
        dot_ref[0, :8, :] = folded(own_psi * own + psi_of(1) * to_next + psi_of(2) * to_prev)
        dot_ref[0, 8:, :] = folded(own_psi * own_psi)


def left_part(two, site, own_env, far_env, psi_rows, base, count):
    lanes = two.shape[2]
    sites = site.shape[0] // M_PAD
    steps = two.shape[1] // (CHUNK * sites * M_PAD)
    block_rows, wide = own_env.shape[0], sites * lanes
    result = pl.BlockSpec((1, block_rows, wide), lambda t, i: (t, 0, 0))
    return pl.pallas_call(
        left_kernel,
        grid=(count, steps),
        in_specs=[
            pl.BlockSpec((1, CHUNK * sites * M_PAD, lanes), lambda t, i: (base + t, i, 0)),
            pl.BlockSpec(site.shape, lambda t, i: (0, 0)),
            pl.BlockSpec((block_rows, CHUNK * M_PAD), lambda t, i: (0, i)),
            pl.BlockSpec((2 * block_rows, CHUNK * M_PAD), lambda t, i: (0, i)),
            pl.BlockSpec((1, 3 * block_rows, wide), lambda t, i: (base + t, 0, 0)),
        ],
        out_specs=[
            result,
            result,
            result,
            pl.BlockSpec((1, 16, wide), lambda t, i: (t, 0, 0)),
        ],
        out_shape=[
            jax.ShapeDtypeStruct((count, block_rows, wide), jnp.float32),
            jax.ShapeDtypeStruct((count, block_rows, wide), jnp.bfloat16),
            jax.ShapeDtypeStruct((count, block_rows, wide), jnp.bfloat16),
            jax.ShapeDtypeStruct((count, 16, wide), jnp.float32),
        ],
        scratch_shapes=[
            pltpu.VMEM((CHUNK * M_PAD, wide), jnp.bfloat16),
            pltpu.VMEM((3 * block_rows, wide), jnp.float32),
        ],
        compiler_params=pltpu.CompilerParams(vmem_limit_bytes=40 * 2**20),
        cost_estimate=pl.CostEstimate(
            flops=2 * count * 3 * block_rows * own_env.shape[1] * wide * 2,
            bytes_accessed=count * (2 * two.shape[1] * lanes + 6 * own_env.size),
            transcendentals=0,
        ),
        name="left_part",
    )(two, site, own_env, far_env, psi_rows)


def neighbours(axis):
    at, count = lax.axis_index(axis), lax.axis_size(axis)
    return at, at > 0, at < count - 1


def place_at(axis, distance):
    row, col = lax.axis_index("row"), lax.axis_index("col")
    return (row + distance, col) if axis == "row" else (row, col + distance)


def remote(source, target, send_sem, recv_sem, place):
    return pltpu.make_async_remote_copy(
        src_ref=source,
        dst_ref=target,
        send_sem=send_sem,
        recv_sem=recv_sem,
        device_id=place,
        device_id_type=pl.DeviceIdType.MESH,
    )


def shift_both(axis, up_ref, down_ref, slots, send_sems, recv_sems):
    _, has_prev, has_next = neighbours(axis)
    up = remote(up_ref, slots.at[0], send_sems.at[0], recv_sems.at[0], place_at(axis, 1))
    down = remote(down_ref, slots.at[1], send_sems.at[1], recv_sems.at[1], place_at(axis, -1))

    def start():
        pl.when(has_next)(up.start)
        pl.when(has_prev)(down.start)

    def finish():
        @pl.when(has_next)
        def _():
            up.wait_send()
            down.wait_recv()

        @pl.when(has_prev)
        def _():
            down.wait_send()
            up.wait_recv()

        @pl.when(jnp.logical_not(has_prev))
        def _():
            slots[0] = jnp.zeros_like(slots[0])

        @pl.when(jnp.logical_not(has_next))
        def _():
            slots[1] = jnp.zeros_like(slots[1])

    return start, finish


def first_kernel(psi_ref, env_ref, psi_out, env_out, psi_slots, env_slots, sends, receives):
    barrier = pltpu.get_barrier_semaphore()
    expected = 0
    for axis in ("row", "col"):
        _, has_prev, has_next = neighbours(axis)
        for there, distance in ((has_prev, -1), (has_next, 1)):
            place = place_at(axis, distance)

            @pl.when(there)
            def _():
                pl.semaphore_signal(
                    barrier, inc=1, device_id=place, device_id_type=pl.DeviceIdType.MESH
                )

            expected = expected + there.astype(jnp.int32)
    pl.semaphore_wait(barrier, expected)
    start_psi, finish_psi = shift_both(
        "col", psi_ref, psi_ref, psi_slots, sends.at[0], receives.at[0]
    )
    start_env, finish_env = shift_both(
        "row", env_ref.at[1], env_ref.at[0], env_slots, sends.at[1], receives.at[1]
    )
    start_env()
    start_psi()
    finish_psi()
    psi_out[...] = psi_slots[...]
    finish_env()
    env_out[...] = env_slots[...]


def vmem_call(kernel, out_shape, scratch_shapes, collective_id, name):
    spec = pl.BlockSpec(memory_space=pltpu.VMEM)
    return pl.pallas_call(
        kernel,
        out_shape=out_shape,
        in_specs=[spec] * (2 if collective_id == 1 else 3),
        out_specs=[spec] * len(out_shape),
        scratch_shapes=scratch_shapes,
        compiler_params=pltpu.CompilerParams(
            collective_id=collective_id, has_side_effects=True, vmem_limit_bytes=32 * 2**20
        ),
        name=name,
    )


def first_moves(psi, env):
    shapes = [(2,) + psi.shape, env.shape]
    return vmem_call(
        first_kernel,
        [jax.ShapeDtypeStruct(shape, jnp.bfloat16) for shape in shapes],
        [pltpu.VMEM(shape, jnp.bfloat16) for shape in shapes]
        + [pltpu.SemaphoreType.DMA((2, 2))] * 2,
        1,
        "first_moves",
    )(psi, env)


def last_kernel(
    sizes, next_ref, prev_ref, dot_ref, sums_out, quotient_out,
    slots, col_slots, row_slots, far_sends, far_receives, sends, receives,
):
    rows, cols = sizes
    row, col = lax.axis_index("row"), lax.axis_index("col")
    lanes = col_slots.shape[2]
    peers = [((row, lax.rem(col + d, cols)), d) for d in range(1, cols)]
    others = [((lax.rem(row + d, rows), col), d) for d in range(1, rows)]
    barrier = pltpu.get_barrier_semaphore()
    for place, _ in peers + others:
        pl.semaphore_signal(barrier, inc=1, device_id=place, device_id_type=pl.DeviceIdType.MESH)
    pl.semaphore_wait(barrier, len(peers) + len(others))

    def exchange(group, buffer, at, offset):
        copies = [
            remote(
                buffer.at[at], buffer.at[at], sends.at[offset + d], receives.at[offset + d], place
            )
            for place, d in group
        ]
        for copy in copies:
            copy.start()
        return copies

    dots = jnp.sum(dot_ref[...], axis=0)
    col_slots[col] = sum(dots[:, at : at + lanes] for at in range(0, dots.shape[1], lanes))
    copies = exchange(peers, col_slots, col, 0)
    start, finish = shift_both("row", next_ref, prev_ref, slots, far_sends, far_receives)
    start()
    for copy in copies:
        copy.wait()
    row_slots[row] = jnp.sum(col_slots[...], axis=0)
    for copy in exchange(others, row_slots, row, cols):
        copy.wait()
    whole = jnp.sum(row_slots[...], axis=0)
    quotient = jnp.sum(whole[:8], keepdims=True) / (jnp.sum(whole[8:], keepdims=True) + 1e-6)
    quotient_out[...] = jnp.broadcast_to(quotient, quotient_out.shape)
    finish()
    sums_out[...] = slots[0].astype(jnp.float32) + slots[1].astype(jnp.float32)


def last_moves(to_next, to_prev, dots, lanes):
    rows, cols = lax.axis_size("row"), lax.axis_size("col")
    return vmem_call(
        functools.partial(last_kernel, (rows, cols)),
        [
            jax.ShapeDtypeStruct(to_next.shape, jnp.float32),
            jax.ShapeDtypeStruct((8, lanes), jnp.float32),
        ],
        [
            pltpu.VMEM((2,) + to_next.shape, jnp.bfloat16),
            pltpu.VMEM((cols, 16, lanes), jnp.float32),
            pltpu.VMEM((rows, 16, lanes), jnp.float32),
            pltpu.SemaphoreType.DMA((2,)),
            pltpu.SemaphoreType.DMA((2,)),
            pltpu.SemaphoreType.DMA((rows + cols,)),
            pltpu.SemaphoreType.DMA((rows + cols,)),
        ],
        2,
        "last_moves",
    )(to_next, to_prev, dots)


def operator_matrix(tensor, narrow):
    width, sites = tensor.shape[0], tensor.shape[2]
    matrix = jnp.pad(
        jnp.transpose(tensor, (2, 0, 3, 1)),
        ((0, 0), (0, M_PAD - width), (0, 0), (0, narrow - width)),
    )
    return matrix.reshape(sites * M_PAD, sites * narrow)


def padded_couplings(coupling):
    lead, width = coupling.shape[:-1], coupling.shape[-1]
    wide = jnp.pad(coupling, [(0, 0)] * len(lead) + [(0, M_PAD - width)])
    return wide.reshape(lead[:-1] + (lead[-1] * M_PAD,))


def on_device(
    psi, env_left, env_right, first_site_operator, mpo_right, block_mask, left_live, right_live
):
    block_rows = env_left.shape[2]
    lanes = env_right.shape[4]
    states = psi.shape[1]
    sites = first_site_operator.shape[2]
    inside = lax.iota(jnp.int32, block_rows)
    live = (
        (block_mask[0, 0] > 0)
        & (inside < left_live[0])[:, None]
        & (lax.iota(jnp.int32, lanes) < right_live[0])[None, :]
    )
    masked = psi * live[:, None, :].astype(jnp.bfloat16)
    flat = masked.reshape(block_rows * states, lanes)
    share = block_rows // lax.axis_size("col")
    shares = lax.dynamic_slice_in_dim(
        env_left[0], lax.axis_index("col") * share, share, 1
    )
    wings = padded_couplings(jnp.stack([shares[0], shares[2]]))
    sides, moved = first_moves(flat, wings)
    moved = moved[::-1].reshape(2 * share, block_rows * M_PAD)
    far_env = lax.all_gather(moved, "col", axis=0, tiled=True)
    own_env = padded_couplings(env_left[0, 1])
    by_t = jnp.transpose(
        masked.reshape(block_rows, sites, sites, lanes), (2, 0, 1, 3)
    ).reshape(sites, block_rows, sites * lanes)
    by_t, sides = lax.optimization_barrier((by_t, sides))
    psi_rows = jnp.concatenate(
        [by_t, from_behind(by_t, "row", -1), from_behind(by_t, "row", 1)], axis=1
    )
    widened = jnp.concatenate([sides[0], flat, sides[1]], axis=1)
    two = right_part(
        widened, jnp.transpose(env_right[0], (0, 2, 1, 3)), operator_matrix(mpo_right, N_PAD)
    )
    first = operator_matrix(first_site_operator, M_PAD)
    half = sites // 2
    own_a, next_a, prev_a, dots_a = left_part(two, first, own_env, far_env, psi_rows, 0, half)
    from_prev = from_behind(next_a, "row", 1)
    from_next = from_behind(prev_a, "row", -1)
    own_b, next_b, prev_b, dots_b = left_part(two, first, own_env, far_env, psi_rows, half, half)
    far_b, ratio = last_moves(next_b, prev_b, jnp.concatenate([dots_a, dots_b]), lanes)
    quotient = ratio[0, 0]
    far_a = from_prev.astype(jnp.float32) + from_next.astype(jnp.float32)
    applied = jnp.concatenate([own_a + far_a, own_b + far_b])
    applied = jnp.transpose(
        applied.reshape(sites, block_rows, sites, lanes), (1, 2, 0, 3)
    ).reshape(block_rows, states, lanes)
    applied = applied * live[:, None, :].astype(jnp.float32)
    return (
        applied.astype(jnp.bfloat16),
        (applied - quotient * masked.astype(jnp.float32)).astype(jnp.bfloat16),
        quotient,
    )


def solution(mesh):
    return jax.shard_map(
        on_device,
        mesh=mesh,
        in_specs=(
            P("row", None, "col"),
            P("row", None, None, None, None),
            P("col", None, None, None, None),
            P(),
            P(),
            P("row", "col"),
            P("row"),
            P("col"),
        ),
        out_specs=(P("row", None, "col"), P("row", None, "col"), P()),
        check_vma=False,
    )
```
